32 devices in a mesh: front: 4 (over z), row: 8 (over y, x, core).
Axes of the slice: x: 2, y: 2, z: 4, core: 2. Of those that a mesh axis runs over, the one named last changes fastest.
Arguments:
- panels: bfloat16 [4, 1024, 1280], P('front', 'row'), may hold values from -6 to 6
- reflectors: bfloat16 [4, 1024, 512], P('front', 'row'), may hold values from -6 to 6
- block_coeffs: bfloat16 [4, 512, 512], P('front')
- block_mask: int32 [4, 8, 4], P('front', 'row'), may hold values 0 or 1
- block_starts: int32 [4, 4], P('front'), may hold values from 0 to 512, as said below
- carry_map: int32 [4, 256], P('front'), may hold values from 0 to 1023, as said below
Outputs:
- panels_out: bfloat16 [4, 1024, 1280], P('front', 'row')
The draws below stay inside these ranges and needn't reach their ends.
Inputs may be any that keep to these rules, and one draw needn't show every extreme that they name: `block_starts`: nondecreasing along the reflector blocks of a front. `carry_map`: within a front the targets are distinct, and carried row i lands in the 128-row block number i % 8, which receives exactly 32 carried rows, its last row among them.
All inputs are finite; a program needn't handle non-finite values. No bound on the sum of `block_mask` on one device may be relied on, other than what follows from the above.
Results may differ from the reference program's by a relative error of at most 0.017.
Values may be sent and summed in bfloat16 or wider, within the bound.
A program may use at most 64 MiB of HBM per device.

```python
import jax
import jax.numpy as jnp

K = 512
RDEV = 128
NC = 1280
ROWS = 1024
FRONTS = 4


def draw_block_coeffs(key, part):
    first_key, second_key = jax.random.split(jax.random.fold_in(key, 7))
    scale_off = 1.0 / (K / 2.0 * (ROWS / 4.0) ** 0.5)
    diagonal = jax.random.uniform(first_key, (FRONTS, K), jnp.float32, 1.0, 2.0) / (ROWS / 4.0)
    offdiag = jax.random.normal(second_key, (FRONTS, K, K), jnp.float32) * scale_off
    upper = jnp.triu(offdiag, 1) + diagonal[:, :, None] * jnp.eye(K, dtype=jnp.float32)[None]
    return upper.astype(jnp.bfloat16)


def draw_block_starts(key, part):
    blocks = K // 128
    raw_starts = jax.random.randint(jax.random.fold_in(key, 11), (FRONTS, blocks), 0, ROWS // 2 + 1)
    sorted_starts = jnp.sort(raw_starts, axis=1)
    columns = jnp.arange(blocks)[None, :]
    fronts_idx = jnp.arange(FRONTS)[:, None]
    sorted_starts = jnp.where((columns == 0) & (fronts_idx == 0), 0, sorted_starts)
    sorted_starts = jnp.where((columns == blocks - 1) & (fronts_idx == FRONTS - 1), ROWS // 2, sorted_starts)
    return sorted_starts.astype(jnp.int32)


def draw_carry_map(key, part):
    row_count = ROWS // RDEV
    per_block = RDEV // 4
    subkeys = jax.random.split(jax.random.fold_in(key, 13), FRONTS * row_count)

    def pick_rows(subkey):
        others = jax.random.permutation(subkey, RDEV - 1)[:per_block - 1].astype(jnp.int32)
        return jnp.concatenate([others, jnp.full((1,), RDEV - 1, jnp.int32)])
    chosen = jax.vmap(pick_rows)(subkeys)
    chosen = chosen.reshape(FRONTS, row_count, per_block).astype(jnp.int32)
    offsets = (jnp.arange(row_count, dtype=jnp.int32) * RDEV)[None, :, None]
    targets = jnp.transpose(chosen + offsets, (0, 2, 1))
    return targets.reshape(FRONTS, per_block * row_count).astype(jnp.int32)


def place_ends(array, key, low, high):
    longest = array.shape.index(max(array.shape))
    spots = []
    for shift in (0, 1):
        where = [jax.random.randint(jax.random.fold_in(key, axis), (), 0, length) for axis, length in enumerate(array.shape)]
        where[longest] = (where[longest] + shift) % array.shape[longest]
        spots.append(tuple(where))
    return array.at[spots[0]].set(low).at[spots[1]].set(high)


def level_of(key, dims, shards, low, top_value):
    loudness, own = 1.0, jax.random.fold_in(key, 6)
    for axis_at, shards_of in shards:
        draws = jnp.exp(jax.random.uniform(jax.random.fold_in(own, axis_at), (shards_of,), jnp.float32, low / len(shards), top_value / len(shards)))
        loudness = loudness * jnp.repeat(draws, dims[axis_at] // shards_of).reshape([-1 if axis == axis_at else 1 for axis in range(len(dims))])
    return loudness


def bell_draw(key, extent, scale, most, cuts=(), kind=jnp.bfloat16):
    array = scale * jax.random.normal(key, extent, jnp.float32)
    if cuts:
        array = array * level_of(key, extent, cuts, -0.22, 0.18)
    return jnp.clip(array, -most, most).astype(kind)


def setup_inputs(seed: int = 0) -> dict:
    arg_keys = jax.random.split(jax.random.key(seed), 7)
    return {
        "panels": bell_draw(arg_keys[0], (FRONTS, ROWS, NC), 1.0, 6.0, ((0, 4), (1, 8))),
        "reflectors": bell_draw(arg_keys[1], (FRONTS, ROWS, K), 1.0, 6.0, ((0, 4), (1, 8))),
        "block_coeffs": draw_block_coeffs(jax.random.fold_in(arg_keys[6], 71), 0),
        "block_mask": place_ends((jax.random.randint(arg_keys[3], (FRONTS, ROWS // 128, K // 128), 0, 2) < 1).astype(jnp.int32), jax.random.fold_in(arg_keys[3], 1), 0, 1),
        "block_starts": draw_block_starts(jax.random.fold_in(arg_keys[6], 71), 0),
        "carry_map": draw_carry_map(jax.random.fold_in(arg_keys[6], 71), 0),
    }


def reference(panels, reflectors, block_coeffs, block_mask, block_starts, carry_map):
    row_ids = jnp.arange(ROWS, dtype=jnp.int32)
    results = []
    carried = None
    for front in range(FRONTS):
        mask_full = jnp.repeat(jnp.repeat(block_mask[front], 128, axis=0), 128, axis=1)
        start_cols = jnp.repeat(block_starts[front], 128)
        retained = (mask_full == 1) & (row_ids[:, None] >= start_cols[None, :])
        effective = jnp.where(retained, reflectors[front], jnp.zeros_like(reflectors[front]))
        assembled = panels[front].astype(jnp.float32)
        if front > 0:
            assembled = assembled.at[carry_map[front]].add(carried.astype(jnp.float32))
        assembled = assembled.astype(jnp.bfloat16)
        partial_value = jnp.dot(effective.T, assembled, preferred_element_type=jnp.float32)
        wcoef = partial_value.astype(jnp.bfloat16)
        mixed = jnp.dot(block_coeffs[front].T, wcoef, preferred_element_type=jnp.float32).astype(jnp.bfloat16)
        result = (assembled.astype(jnp.float32) - jnp.dot(effective, mixed, preferred_element_type=jnp.float32)).astype(jnp.bfloat16)
        results.append(result)
        carried = result[3 * ROWS // 4:]
    return jnp.stack(results)
```

```python
import functools

import jax
import jax.numpy as jnp
from jax import lax
from jax.experimental import pallas as pl
from jax.experimental.pallas import tpu as pltpu
from jax.sharding import PartitionSpec as P

F32 = jnp.float32
BF16 = jnp.bfloat16
LANES = 128


def dot(a, b):
    return jnp.dot(a, b, preferred_element_type=F32)


def dot_nt(a, b):
    return lax.dot_general(a, b, (((1,), (1,)), ((), ())), preferred_element_type=F32)


def kernel(
    n, fronts, width,
    mask_ref, starts_ref, panels_ref, refl_ref, coeffs_ref, cmap_ref, out_ref,
    pt, pr, ea, place, ec, cin, sacc, rt, rr,
    e_send, e_recv, s_send, s_recv, p_send, p_recv, r_send, r_recv, z_send, z_recv,
):
    me = lax.axis_index("row")
    front = lax.axis_index("front")
    span = panels_ref.shape[1]
    cols = panels_ref.shape[2]
    rows = n * span
    tail = 3 * rows // 4
    chips = n // 2
    chip = me // 2
    core = me % 2
    sibling = chip * 2 + (1 - core)

    def at_row(r):
        return {"front": front, "row": r}

    def at_front(f):
        return {"front": f, "row": me}

    def remote(src, dst, ss, rs, dev):
        return pltpu.make_async_remote_copy(
            src_ref=src, dst_ref=dst, send_sem=ss, recv_sem=rs,
            device_id=dev, device_id_type=pl.DeviceIdType.MESH,
        )

    def blk(r):
        return pl.ds(pl.multiple_of(r * span, span), span)

    def strip(r):
        return pl.ds(pl.multiple_of(r * width, 16), width)

    barrier = pltpu.get_barrier_semaphore()
    for k in range(1, n):
        pl.semaphore_signal(barrier, inc=1, device_id=at_row((me + k) % n),
                            device_id_type=pl.DeviceIdType.MESH)

    @pl.when(front > 0)
    def _():
        pl.semaphore_signal(barrier, inc=1, device_id=at_front(front - 1),
                            device_id_type=pl.DeviceIdType.MESH)

    @pl.when(front < fronts - 1)
    def _():
        pl.semaphore_signal(barrier, inc=1, device_id=at_front(front + 1),
                            device_id_type=pl.DeviceIdType.MESH)

    row_ids = me * span + lax.broadcasted_iota(jnp.int32, (span, LANES), 0)
    for j in range(refl_ref.shape[2] // LANES):
        keep = jnp.logical_and(row_ids >= starts_ref[0, j], mask_ref[0, 0, j] == 1)
        block = refl_ref[0, :, j * LANES:(j + 1) * LANES]
        ea[blk(me), j * LANES:(j + 1) * LANES] = jnp.where(keep, block, jnp.zeros_like(block))

    pl.semaphore_wait(barrier, n - 1 + jnp.where(front > 0, 1, 0)
                      + jnp.where(front < fronts - 1, 1, 0))

    e_out = []
    for k in range(1, chips):
        c = remote(ea.at[blk(me)], ea.at[blk(me)], e_send.at[k], e_recv.at[k],
                   at_row(((chip + k) % chips) * 2 + core))
        c.start()
        e_out.append(c)
    c = remote(ea.at[blk(me)], ea.at[blk(me)], s_send.at[0], s_recv.at[0], at_row(sibling))
    c.start()
    e_out.append(c)

    for j in range(cols // LANES):
        pt[j * LANES:(j + 1) * LANES, :] = panels_ref[0, :, j * LANES:(j + 1) * LANES].T
    if pt.shape[0] > cols:
        pt[cols:, :] = jnp.zeros((pt.shape[0] - cols, span), BF16)
    p_out = []
    for k in range(1, n):
        peer = (me + k) % n
        c = remote(pt.at[strip(peer)], pr.at[:, blk(me)], p_send.at[k], p_recv.at[k], at_row(peer))
        c.start()
        p_out.append(c)
    pr[:, blk(me)] = pt[strip(me), :]

    ncar = cmap_ref.shape[1]
    targets = jnp.broadcast_to(cmap_ref[...], (LANES, ncar)).T
    lane = lax.broadcasted_iota(jnp.int32, (ncar, LANES), 1)
    for b in range(rows // LANES):
        place[:, b * LANES:(b + 1) * LANES] = jnp.where(
            targets == lane + b * LANES, 1.0, 0.0).astype(BF16)

    for k in range(1, chips):
        src = ((chip + chips - k) % chips) * 2 + core
        e_out[k - 1].wait_recv()
        c = remote(ea.at[blk(src)], ea.at[blk(src)], s_send.at[k], s_recv.at[k], at_row(sibling))
        c.start()
        e_out.append(c)
    for c in e_out[chips - 1:]:
        c.wait_recv()

    ec[...] = dot(place[...], ea[...]).astype(BF16)

    for c in p_out:
        c.wait_recv()
    sacc[...] = dot(pr[...], ea[...])

    z_copy = remote(rt.at[:, pl.ds(tail, rows - tail)], cin, z_send, z_recv,
                    at_front((front + 1) % fronts))

    @pl.when(front == 0)
    def _():
        cin[...] = jnp.zeros_like(cin)

    @pl.when(front > 0)
    def _():
        z_copy.wait_recv()

    carried = cin[...]
    wcoef = (sacc[...] + dot(carried, ec[...])).astype(BF16)
    mixed = dot(wcoef, coeffs_ref[0]).astype(BF16)

    def finish(lo, hi):
        assembled = (pr[:, lo:hi].astype(F32) + dot(carried, place[:, lo:hi])).astype(BF16)
        rt[:, lo:hi] = (assembled.astype(F32) - dot_nt(mixed, ea[lo:hi, :])).astype(BF16)

    finish(tail, rows)

    @pl.when(front < fronts - 1)
    def _():
        z_copy.start()

    finish(0, tail)

    r_out = []
    for k in range(1, n):
        peer = (me + k) % n
        c = remote(rt.at[:, blk(peer)], rr.at[strip(me)], r_send.at[k], r_recv.at[k], at_row(peer))
        c.start()
        r_out.append(c)
    rr[strip(me), :] = rt[:, blk(me)]
    for c in r_out:
        c.wait_recv()
    for j in range(cols // LANES):
        out_ref[0, :, j * LANES:(j + 1) * LANES] = rr[j * LANES:(j + 1) * LANES, :].T

    for c in e_out + p_out + r_out:
        c.wait_send()

    @pl.when(front < fronts - 1)
    def _():
        z_copy.wait_send()


def local(n, fronts, panels, reflectors, block_coeffs, block_mask, block_starts, carry_map):
    _, span, cols = panels.shape
    k = reflectors.shape[2]
    rows = n * span
    ncar = carry_map.shape[1]
    width = -(-cols // (16 * n)) * 16
    dma = pltpu.SemaphoreType.DMA
    vmem = pl.BlockSpec(memory_space=pltpu.VMEM)
    smem = pl.BlockSpec(memory_space=pltpu.SMEM)
    return pl.pallas_call(
        functools.partial(kernel, n, fronts, width),
        out_shape=jax.ShapeDtypeStruct(panels.shape, panels.dtype),
        in_specs=[smem, smem, vmem, vmem, vmem, vmem],
        out_specs=vmem,
        scratch_shapes=[
            pltpu.VMEM((n * width, span), BF16),
            pltpu.VMEM((width, rows), BF16),
            pltpu.VMEM((rows, k), BF16),
            pltpu.VMEM((ncar, rows), BF16),
            pltpu.VMEM((ncar, k), BF16),
            pltpu.VMEM((width, ncar), BF16),
            pltpu.VMEM((width, k), F32),
            pltpu.VMEM((width, rows), BF16),
            pltpu.VMEM((n * width, span), BF16),
            dma((n // 2,)), dma((n // 2,)), dma((n // 2,)), dma((n // 2,)),
            dma((n,)), dma((n,)), dma((n,)), dma((n,)), dma, dma,
        ],
        compiler_params=pltpu.CompilerParams(
            collective_id=0, has_side_effects=True, vmem_limit_bytes=48 * 1024 * 1024),
    )(block_mask, block_starts, panels, reflectors, block_coeffs, carry_map)


def solution(mesh):
    in_specs = (
        P("front", "row", None),
        P("front", "row", None),
        P("front", None, None),
        P("front", "row", None),
        P("front", None),
        P("front", None),
    )
    body = functools.partial(local, mesh.shape["row"], mesh.shape["front"])
    return jax.shard_map(body, mesh=mesh, in_specs=in_specs,
                         out_specs=P("front", "row", None), check_vma=False)
```

```python
import functools

import jax
import jax.numpy as jnp
from jax import lax
from jax.experimental import pallas as pl
from jax.experimental.pallas import tpu as pltpu
from jax.sharding import PartitionSpec as P

F32 = jnp.float32
BF16 = jnp.bfloat16
LANES = 128


def dot(a, b):
    return jnp.dot(a, b, preferred_element_type=F32)


def dot_nt(a, b):
    return lax.dot_general(a, b, (((1,), (1,)), ((), ())), preferred_element_type=F32)


def kernel(
    n, fronts, bounds, width,
    mask_hbm, starts_hbm, panels_hbm, refl_hbm, coeffs_hbm, cmap_hbm, out_ref,
    mask, starts, panels, refl, coeffs, cmap,
    pt, pr, ea, place, ec, step, step_in, tails, tail_in, cout, cin, carry, sacc, rt, rr,
    in_sem, e_send, e_recv, s_send, s_recv, p_send, p_recv, r_send, r_recv,
    t_send, t_recv, c_send, d_send, c_recv, m_send, m_recv,
):
    me = lax.axis_index("row")
    front = lax.axis_index("front")
    span = panels.shape[1]
    cols = panels.shape[2]
    rows = n * span
    tail = 3 * rows // 4
    chips = n // 2
    chip = me // 2
    core = me % 2
    sibling = chip * 2 + (1 - core)
    mesh_id = pl.DeviceIdType.MESH

    def at_row(r):
        return {"front": front, "row": r}

    def at_front(f):
        return {"front": f, "row": me}

    def remote(src, dst, ss, rs, dev):
        return pltpu.make_async_remote_copy(
            src_ref=src, dst_ref=dst, send_sem=ss, recv_sem=rs,
            device_id=dev, device_id_type=mesh_id,
        )

    def blk(r):
        return pl.ds(pl.multiple_of(r * span, span), span)

    def strip(r, lo, hi):
        return pl.ds(pl.multiple_of(r * width + lo, 16), hi - lo)

    loads = [
        pltpu.make_async_copy(src, dst, in_sem.at[i])
        for i, (src, dst) in enumerate([
            (mask_hbm, mask), (starts_hbm, starts), (refl_hbm, refl),
            (panels_hbm, panels), (cmap_hbm, cmap), (coeffs_hbm, coeffs)])
    ]
    for load in loads:
        load.start()

    barrier = pltpu.get_barrier_semaphore()
    for k in range(1, n):
        pl.semaphore_signal(barrier, inc=1, device_id=at_row((me + k) % n),
                            device_id_type=mesh_id)
    greeted = n - 1
    for d in (-2, -1, 1, 2):
        there = jnp.logical_and(front + d >= 0, front + d < fronts)
        greeted = greeted + jnp.where(there, 1, 0)

        @pl.when(there)
        def _(d=d):
            pl.semaphore_signal(barrier, inc=1, device_id=at_front(front + d),
                                device_id_type=mesh_id)

    for load in loads[:3]:
        load.wait()
    row_ids = me * span + lax.broadcasted_iota(jnp.int32, (span, LANES), 0)
    for j in range(refl.shape[2] // LANES):
        keep = jnp.logical_and(row_ids >= starts[0, j], mask[0, 0, j] == 1)
        block = refl[0, :, j * LANES:(j + 1) * LANES]
        ea[blk(me), j * LANES:(j + 1) * LANES] = jnp.where(keep, block, jnp.zeros_like(block))

    pl.semaphore_wait(barrier, greeted)

    e_out = []
    for k in range(1, chips):
        c = remote(ea.at[blk(me)], ea.at[blk(me)], e_send.at[k], e_recv.at[k],
                   at_row(((chip + k) % chips) * 2 + core))
        c.start()
        e_out.append(c)
    c = remote(ea.at[blk(me)], ea.at[blk(me)], s_send.at[0], s_recv.at[0], at_row(sibling))
    c.start()
    e_out.append(c)

    loads[3].wait()
    for j in range(cols // LANES):
        pt[j * LANES:(j + 1) * LANES, :] = panels[0, :, j * LANES:(j + 1) * LANES].T
    if pt.shape[0] > cols:
        pt[cols:, :] = jnp.zeros((pt.shape[0] - cols, span), BF16)
    p_out = []
    for h, (lo, hi) in enumerate(bounds):
        for k in range(1, n):
            peer = (me + k) % n
            c = remote(pt.at[strip(peer, lo, hi)], pr.at[pl.ds(lo, hi - lo), blk(me)],
                       p_send.at[h, k], p_recv.at[h, k], at_row(peer))
            c.start()
            p_out.append(c)
    pr[:, blk(me)] = pt[strip(me, 0, width), :]

    loads[4].wait()
    ncar = cmap.shape[1]
    targets = jnp.broadcast_to(cmap[...], (LANES, ncar)).T
    lane = lax.broadcasted_iota(jnp.int32, (ncar, LANES), 1)
    for b in range(rows // LANES):
        place[:, b * LANES:(b + 1) * LANES] = jnp.where(
            targets == lane + b * LANES, 1.0, 0.0).astype(BF16)
    loads[5].wait()

    for k in range(1, chips):
        src = ((chip + chips - k) % chips) * 2 + core
        e_out[k - 1].wait_recv()
        c = remote(ea.at[blk(src)], ea.at[blk(src)], s_send.at[k], s_recv.at[k], at_row(sibling))
        c.start()
        e_out.append(c)
    for c in e_out[chips - 1:]:
        c.wait_recv()

    ec[...] = dot(place[...], ea[...]).astype(BF16)
    through = dot(ec[...], coeffs[0]).astype(BF16)
    step[...] = (place[:, tail:].astype(F32) - dot_nt(through, ea[tail:, :])).astype(BF16)

    even = front % 2 == 0
    has_next = front + 1 < fronts
    feeds = jnp.logical_and(even, has_next)
    feeds_map = jnp.logical_and(feeds, front > 0)
    odd_next = jnp.logical_and(front % 2 == 1, has_next)
    odd_after = jnp.logical_and(front % 2 == 1, front + 2 < fronts)
    odd_late = jnp.logical_and(front % 2 == 1, front > 1)
    even_late = jnp.logical_and(even, front > 0)

    m_copy = remote(step, step_in, m_send, m_recv, at_front(lax.rem(front + 1, fronts)))

    @pl.when(feeds_map)
    def _():
        m_copy.start()

    t_copies, c_copies, d_copies, r_out = [], [], [], []
    for h, (lo, hi) in enumerate(bounds):
        part = pl.ds(lo, hi - lo)
        t_copies.append(remote(tails.at[part], tail_in.at[part], t_send.at[h], t_recv.at[h],
                               at_front(lax.rem(front + 1, fronts))))
        c_copies.append(remote(cout.at[part], cin.at[part], c_send.at[h], c_recv.at[h],
                               at_front(lax.rem(front + 1, fronts))))
        d_copies.append(remote(cout.at[part], cin.at[part], d_send.at[h], c_recv.at[h],
                               at_front(lax.rem(front + 2, fronts))))

    for h, (lo, hi) in enumerate(bounds):
        for c in p_out[h * (n - 1):(h + 1) * (n - 1)]:
            c.wait_recv()
        total = dot(pr[lo:hi, :], ea[...])
        sacc[lo:hi, :] = total
        mixed = dot(total.astype(BF16), coeffs[0]).astype(BF16)
        tails[lo:hi, :] = (
            pr[lo:hi, tail:].astype(F32) - dot_nt(mixed, ea[tail:, :])).astype(BF16)

        @pl.when(feeds)
        def _(h=h):
            t_copies[h].start()

    for h, (lo, hi) in enumerate(bounds):
        @pl.when(front == 0)
        def _():
            carry[lo:hi, :] = jnp.zeros((hi - lo, ncar), BF16)

        @pl.when(front == 1)
        def _():
            t_copies[h].wait_recv()
            carry[lo:hi, :] = tail_in[lo:hi, :]

        @pl.when(even_late)
        def _():
            c_copies[h].wait_recv()
            carry[lo:hi, :] = cin[lo:hi, :]

        @pl.when(odd_late)
        def _():
            if h == 0:
                m_copy.wait_recv()
            t_copies[h].wait_recv()
            c_copies[h].wait_recv()
            carry[lo:hi, :] = (tail_in[lo:hi, :].astype(F32)
                               + dot(cin[lo:hi, :], step_in[...])).astype(BF16)

        @pl.when(odd_next)
        def _():
            cout[lo:hi, :] = (tails[lo:hi, :].astype(F32)
                              + dot(carry[lo:hi, :], step[...])).astype(BF16)

        @pl.when(odd_after)
        def _():
            d_copies[h].start()

        @pl.when(odd_next)
        def _():
            c_copies[h].start()

        carried = carry[lo:hi, :]
        wcoef = (sacc[lo:hi, :] + dot(carried, ec[...])).astype(BF16)
        mixed = dot(wcoef, coeffs[0]).astype(BF16)
        assembled = (pr[lo:hi, :].astype(F32) + dot(carried, place[...])).astype(BF16)
        rt[lo:hi, :] = (assembled.astype(F32) - dot_nt(mixed, ea[...])).astype(BF16)
        for k in range(1, n):
            peer = (me + k) % n
            c = remote(rt.at[pl.ds(lo, hi - lo), blk(peer)], rr.at[strip(me, lo, hi)],
                       r_send.at[h, k], r_recv.at[h, k], at_row(peer))
            c.start()
            r_out.append(c)
        rr[strip(me, lo, hi), :] = rt[lo:hi, blk(me)]

    for c in r_out:
        c.wait_recv()
    for j in range(cols // LANES):
        out_ref[0, :, j * LANES:(j + 1) * LANES] = rr[j * LANES:(j + 1) * LANES, :].T

    for c in e_out + p_out + r_out:
        c.wait_send()
    for flag, copies in ((feeds_map, [m_copy]), (feeds, t_copies),
                         (odd_after, d_copies), (odd_next, c_copies)):
        @pl.when(flag)
        def _(copies=copies):
            for c in copies:
                c.wait_send()


def local(n, fronts, panels, reflectors, block_coeffs, block_mask, block_starts, carry_map):
    _, span, cols = panels.shape
    k = reflectors.shape[2]
    rows = n * span
    ncar = carry_map.shape[1]
    width = -(-cols // (16 * n)) * 16
    half = width // 32 * 16
    bounds = ((0, half), (half, width))
    parts = len(bounds)
    dma = pltpu.SemaphoreType.DMA
    hbm = pl.BlockSpec(memory_space=pltpu.HBM)
    return pl.pallas_call(
        functools.partial(kernel, n, fronts, bounds, width),
        out_shape=jax.ShapeDtypeStruct(panels.shape, panels.dtype),
        in_specs=[hbm] * 6,
        out_specs=pl.BlockSpec(memory_space=pltpu.VMEM),
        scratch_shapes=[
            pltpu.SMEM(block_mask.shape, jnp.int32),
            pltpu.SMEM(block_starts.shape, jnp.int32),
            pltpu.VMEM(panels.shape, BF16),
            pltpu.VMEM(reflectors.shape, BF16),
            pltpu.VMEM(block_coeffs.shape, BF16),
            pltpu.VMEM(carry_map.shape, jnp.int32),
            pltpu.VMEM((n * width, span), BF16),
            pltpu.VMEM((width, rows), BF16),
            pltpu.VMEM((rows, k), BF16),
            pltpu.VMEM((ncar, rows), BF16),
            pltpu.VMEM((ncar, k), BF16),
            pltpu.VMEM((ncar, ncar), BF16),
            pltpu.VMEM((ncar, ncar), BF16),
            pltpu.VMEM((width, ncar), BF16),
            pltpu.VMEM((width, ncar), BF16),
            pltpu.VMEM((width, ncar), BF16),
            pltpu.VMEM((width, ncar), BF16),
            pltpu.VMEM((width, ncar), BF16),
            pltpu.VMEM((width, k), F32),
            pltpu.VMEM((width, rows), BF16),
            pltpu.VMEM((n * width, span), BF16),
            dma((6,)),
            dma((n // 2,)), dma((n // 2,)), dma((n // 2,)), dma((n // 2,)),
            dma((parts, n)), dma((parts, n)), dma((parts, n)), dma((parts, n)),
            dma((parts,)), dma((parts,)), dma((parts,)), dma((parts,)), dma((parts,)),
            dma, dma,
        ],
        compiler_params=pltpu.CompilerParams(
            collective_id=0, has_side_effects=True, vmem_limit_bytes=56 * 1024 * 1024),
    )(block_mask, block_starts, panels, reflectors, block_coeffs, carry_map)


def solution(mesh):
    in_specs = (
        P("front", "row", None),
        P("front", "row", None),
        P("front", None, None),
        P("front", "row", None),
        P("front", None),
        P("front", None),
    )
    body = functools.partial(local, mesh.shape["row"], mesh.shape["front"])
    return jax.shard_map(body, mesh=mesh, in_specs=in_specs,
                         out_specs=P("front", "row", None), check_vma=False)
```

```python
import functools

import jax
import jax.numpy as jnp
from jax import lax
from jax.experimental import pallas as pl
from jax.experimental.pallas import tpu as pltpu
from jax.sharding import PartitionSpec as P

F32 = jnp.float32
BF16 = jnp.bfloat16
LANES = 128


def dot(a, b):
    return jnp.dot(a, b, preferred_element_type=F32)


def dot_nt(a, b):
    return lax.dot_general(a, b, (((1,), (1,)), ((), ())), preferred_element_type=F32)


def kernel(
    n, fronts, bounds, width,
    mask_hbm, starts_hbm, panels_hbm, refl_hbm, coeffs_hbm, cmap_hbm, out_ref,
    mask, starts, panels, refl, coeffs, cmap,
    pt, pr, ea, place, step, step_in, tails, tail_in, cout, cin, carry, mix, rest, rt, rr,
    in_sem, e_send, e_recv, s_send, s_recv, p_send, p_recv, r_send, r_recv,
    t_send, t_recv, c_send, d_send, c_recv, m_send, m_recv,
):
    me = lax.axis_index("row")
    front = lax.axis_index("front")
    span = panels.shape[1]
    cols = panels.shape[2]
    rows = n * span
    tail = 3 * rows // 4
    chips = n // 2
    chip = me // 2
    core = me % 2
    sibling = chip * 2 + (1 - core)
    mesh_id = pl.DeviceIdType.MESH

    def at_row(r):
        return {"front": front, "row": r}

    def at_front(f):
        return {"front": f, "row": me}

    def remote(src, dst, ss, rs, dev):
        return pltpu.make_async_remote_copy(
            src_ref=src, dst_ref=dst, send_sem=ss, recv_sem=rs,
            device_id=dev, device_id_type=mesh_id,
        )

    def blk(r):
        return pl.ds(pl.multiple_of(r * span, span), span)

    def strip(r, lo, hi):
        return pl.ds(pl.multiple_of(r * width + lo, 16), hi - lo)

    loads = [
        pltpu.make_async_copy(src, dst, in_sem.at[i])
        for i, (src, dst) in enumerate([
            (mask_hbm, mask), (starts_hbm, starts), (refl_hbm, refl),
            (panels_hbm, panels), (cmap_hbm, cmap), (coeffs_hbm, coeffs)])
    ]
    for load in loads:
        load.start()

    barrier = pltpu.get_barrier_semaphore()
    for k in range(1, n):
        pl.semaphore_signal(barrier, inc=1, device_id=at_row((me + k) % n),
                            device_id_type=mesh_id)
    greeted = n - 1
    for d in (-2, -1, 1, 2):
        there = jnp.logical_and(front + d >= 0, front + d < fronts)
        greeted = greeted + jnp.where(there, 1, 0)

        @pl.when(there)
        def _(d=d):
            pl.semaphore_signal(barrier, inc=1, device_id=at_front(front + d),
                                device_id_type=mesh_id)

    for load in loads[:3]:
        load.wait()
    row_ids = me * span + lax.broadcasted_iota(jnp.int32, (span, LANES), 0)
    for j in range(refl.shape[2] // LANES):
        keep = jnp.logical_and(row_ids >= starts[0, j], mask[0, 0, j] == 1)
        block = refl[0, :, j * LANES:(j + 1) * LANES]
        ea[blk(me), j * LANES:(j + 1) * LANES] = jnp.where(keep, block, jnp.zeros_like(block))

    pl.semaphore_wait(barrier, greeted)

    e_out = []
    for k in range(1, chips):
        c = remote(ea.at[blk(me)], ea.at[blk(me)], e_send.at[k], e_recv.at[k],
                   at_row(((chip + k) % chips) * 2 + core))
        c.start()
        e_out.append(c)
    c = remote(ea.at[blk(me)], ea.at[blk(me)], s_send.at[0], s_recv.at[0], at_row(sibling))
    c.start()
    e_out.append(c)

    loads[3].wait()
    for j in range(cols // LANES):
        pt[j * LANES:(j + 1) * LANES, :] = panels[0, :, j * LANES:(j + 1) * LANES].T
    if pt.shape[0] > cols:
        pt[cols:, :] = jnp.zeros((pt.shape[0] - cols, span), BF16)
    p_out = []
    for h, (lo, hi) in enumerate(bounds):
        for k in range(1, n):
            peer = (me + k) % n
            c = remote(pt.at[strip(peer, lo, hi)], pr.at[pl.ds(lo, hi - lo), blk(me)],
                       p_send.at[h, k], p_recv.at[h, k], at_row(peer))
            c.start()
            p_out.append(c)
    pr[:, blk(me)] = pt[strip(me, 0, width), :]

    loads[4].wait()
    ncar = cmap.shape[1]
    targets = jnp.broadcast_to(cmap[...], (LANES, ncar)).T
    lane = lax.broadcasted_iota(jnp.int32, (ncar, LANES), 1)
    for b in range(rows // LANES):
        place[:, b * LANES:(b + 1) * LANES] = jnp.where(
            targets == lane + b * LANES, 1.0, 0.0).astype(BF16)
    loads[5].wait()

    for k in range(1, chips):
        src = ((chip + chips - k) % chips) * 2 + core
        e_out[k - 1].wait_recv()
        c = remote(ea.at[blk(src)], ea.at[blk(src)], s_send.at[k], s_recv.at[k], at_row(sibling))
        c.start()
        e_out.append(c)
    for c in e_out[chips - 1:]:
        c.wait_recv()

    even = front % 2 == 0
    has_next = front + 1 < fronts
    feeds = jnp.logical_and(even, has_next)
    feeds_map = jnp.logical_and(feeds, front > 0)
    odd_next = jnp.logical_and(front % 2 == 1, has_next)
    odd_after = jnp.logical_and(front % 2 == 1, front + 2 < fronts)
    odd_late = jnp.logical_and(front % 2 == 1, front > 1)
    even_late = jnp.logical_and(even, front > 0)

    m_copy = remote(step.at[:, pl.ds(tail, rows - tail)], step_in, m_send, m_recv,
                    at_front(lax.rem(front + 1, fronts)))

    t_copies, c_copies, d_copies, r_out = [], [], [], []
    for h, (lo, hi) in enumerate(bounds):
        part = pl.ds(lo, hi - lo)
        t_copies.append(remote(tails.at[part], tail_in.at[part], t_send.at[h], t_recv.at[h],
                               at_front(lax.rem(front + 1, fronts))))
        c_copies.append(remote(cout.at[part], cin.at[part], c_send.at[h], c_recv.at[h],
                               at_front(lax.rem(front + 1, fronts))))
        d_copies.append(remote(cout.at[part], cin.at[part], d_send.at[h], c_recv.at[h],
                               at_front(lax.rem(front + 2, fronts))))

    for h, (lo, hi) in enumerate(bounds):
        for c in p_out[h * (n - 1):(h + 1) * (n - 1)]:
            c.wait_recv()
        wcoef = dot(pr[lo:hi, :], ea[...]).astype(BF16)
        mix[lo:hi, :] = dot(wcoef, coeffs[0]).astype(BF16)
        own = pr[lo:hi, tail:].astype(F32) - dot_nt(mix[lo:hi, :], ea[tail:, :])
        tails[lo:hi, :] = own.astype(BF16)
        rest[lo:hi, tail:] = own

        @pl.when(feeds)
        def _(h=h):
            t_copies[h].start()

    ec = dot(place[...], ea[...]).astype(BF16)
    through = dot(ec, coeffs[0]).astype(BF16)

    def map_columns(lo, hi):
        step[:, lo:hi] = (place[:, lo:hi].astype(F32)
                          - dot_nt(through, ea[lo:hi, :])).astype(BF16)

    map_columns(tail, rows)

    @pl.when(feeds_map)
    def _():
        m_copy.start()

    def rest_rows(lo, hi):
        rest[lo:hi, :tail] = pr[lo:hi, :tail].astype(F32) - dot_nt(mix[lo:hi, :], ea[:tail, :])

    @pl.when(front == 0)
    def _():
        for lo, hi in bounds:
            rest_rows(lo, hi)

    @pl.when(front > 0)
    def _():
        map_columns(0, tail)
        rest_rows(0, width)

    for h, (lo, hi) in enumerate(bounds):
        @pl.when(front == 1)
        def _():
            t_copies[h].wait_recv()
            carry[lo:hi, :] = tail_in[lo:hi, :]

        @pl.when(even_late)
        def _():
            c_copies[h].wait_recv()
            carry[lo:hi, :] = cin[lo:hi, :]

        @pl.when(odd_late)
        def _():
            if h == 0:
                m_copy.wait_recv()
            t_copies[h].wait_recv()
            c_copies[h].wait_recv()
            carry[lo:hi, :] = (tail_in[lo:hi, :].astype(F32)
                               + dot(cin[lo:hi, :], step_in[...])).astype(BF16)

        @pl.when(odd_next)
        def _():
            cout[lo:hi, :] = (tails[lo:hi, :].astype(F32)
                              + dot(carry[lo:hi, :], step[:, tail:])).astype(BF16)

        @pl.when(odd_after)
        def _():
            d_copies[h].start()

        @pl.when(odd_next)
        def _():
            c_copies[h].start()

        @pl.when(front == 0)
        def _():
            rt[lo:hi, :] = rest[lo:hi, :].astype(BF16)

        @pl.when(front > 0)
        def _():
            rt[lo:hi, :] = (rest[lo:hi, :] + dot(carry[lo:hi, :], step[...])).astype(BF16)

        for k in range(1, n):
            peer = (me + k) % n
            c = remote(rt.at[pl.ds(lo, hi - lo), blk(peer)], rr.at[strip(me, lo, hi)],
                       r_send.at[h, k], r_recv.at[h, k], at_row(peer))
            c.start()
            r_out.append(c)
        rr[strip(me, lo, hi), :] = rt[lo:hi, blk(me)]

    for c in r_out:
        c.wait_recv()
    for j in range(cols // LANES):
        out_ref[0, :, j * LANES:(j + 1) * LANES] = rr[j * LANES:(j + 1) * LANES, :].T

    for c in e_out + p_out + r_out:
        c.wait_send()
    for flag, copies in ((feeds_map, [m_copy]), (feeds, t_copies),
                         (odd_after, d_copies), (odd_next, c_copies)):
        @pl.when(flag)
        def _(copies=copies):
            for c in copies:
                c.wait_send()


def local(n, fronts, panels, reflectors, block_coeffs, block_mask, block_starts, carry_map):
    _, span, cols = panels.shape
    k = reflectors.shape[2]
    rows = n * span
    ncar = carry_map.shape[1]
    width = -(-cols // (16 * n)) * 16
    half = width // 32 * 16
    bounds = ((0, half), (half, width))
    parts = len(bounds)
    dma = pltpu.SemaphoreType.DMA
    hbm = pl.BlockSpec(memory_space=pltpu.HBM)
    return pl.pallas_call(
        functools.partial(kernel, n, fronts, bounds, width),
        out_shape=jax.ShapeDtypeStruct(panels.shape, panels.dtype),
        in_specs=[hbm] * 6,
        out_specs=pl.BlockSpec(memory_space=pltpu.VMEM),
        scratch_shapes=[
            pltpu.SMEM(block_mask.shape, jnp.int32),
            pltpu.SMEM(block_starts.shape, jnp.int32),
            pltpu.VMEM(panels.shape, BF16),
            pltpu.VMEM(reflectors.shape, BF16),
            pltpu.VMEM(block_coeffs.shape, BF16),
            pltpu.VMEM(carry_map.shape, jnp.int32),
            pltpu.VMEM((n * width, span), BF16),
            pltpu.VMEM((width, rows), BF16),
            pltpu.VMEM((rows, k), BF16),
            pltpu.VMEM((ncar, rows), BF16),
            pltpu.VMEM((ncar, rows), BF16),
            pltpu.VMEM((ncar, ncar), BF16),
            pltpu.VMEM((width, ncar), BF16),
            pltpu.VMEM((width, ncar), BF16),
            pltpu.VMEM((width, ncar), BF16),
            pltpu.VMEM((width, ncar), BF16),
            pltpu.VMEM((width, ncar), BF16),
            pltpu.VMEM((width, k), BF16),
            pltpu.VMEM((width, rows), F32),
            pltpu.VMEM((width, rows), BF16),
            pltpu.VMEM((n * width, span), BF16),
            dma((6,)),
            dma((n // 2,)), dma((n // 2,)), dma((n // 2,)), dma((n // 2,)),
            dma((parts, n)), dma((parts, n)), dma((parts, n)), dma((parts, n)),
            dma((parts,)), dma((parts,)), dma((parts,)), dma((parts,)), dma((parts,)),
            dma, dma,
        ],
        compiler_params=pltpu.CompilerParams(
            collective_id=0, has_side_effects=True, vmem_limit_bytes=56 * 1024 * 1024),
    )(block_mask, block_starts, panels, reflectors, block_coeffs, carry_map)


def solution(mesh):
    in_specs = (
        P("front", "row", None),
        P("front", "row", None),
        P("front", None, None),
        P("front", "row", None),
        P("front", None),
        P("front", None),
    )
    body = functools.partial(local, mesh.shape["row"], mesh.shape["front"])
    return jax.shard_map(body, mesh=mesh, in_specs=in_specs,
                         out_specs=P("front", "row", None), check_vma=False)
```

```python
import functools

import jax
import jax.numpy as jnp
from jax import lax
from jax.experimental import pallas as pl
from jax.experimental.pallas import tpu as pltpu
from jax.sharding import PartitionSpec as P

F32 = jnp.float32
BF16 = jnp.bfloat16
LANES = 128


def dot(a, b):
    return jnp.dot(a, b, preferred_element_type=F32)


def dot_nt(a, b):
    return lax.dot_general(a, b, (((1,), (1,)), ((), ())), preferred_element_type=F32)


def kernel(
    n, fronts, bounds, width,
    mask_hbm, starts_hbm, panels_hbm, refl_hbm, coeffs_hbm, cmap_hbm, out_ref,
    mask, starts, panels, refl, coeffs, cmap,
    pt, pr, ea, place, step, step_in, tails, tail_in, cout, cin, carry, mix, rest, rt, rr,
    in_sem, e_send, e_recv, s_send, s_recv, p_send, p_recv, r_send, r_recv,
    t_send, t_recv, c_send, d_send, c_recv, m_send, m_recv,
):
    me = lax.axis_index("row")
    front = lax.axis_index("front")
    span = panels.shape[1]
    cols = panels.shape[2]
    rows = n * span
    tail = 3 * rows // 4
    chips = n // 2
    chip = me // 2
    core = me % 2
    sibling = chip * 2 + (1 - core)
    mesh_id = pl.DeviceIdType.MESH

    def at_row(r):
        return {"front": front, "row": r}

    def at_front(f):
        return {"front": f, "row": me}

    def remote(src, dst, ss, rs, dev):
        return pltpu.make_async_remote_copy(
            src_ref=src, dst_ref=dst, send_sem=ss, recv_sem=rs,
            device_id=dev, device_id_type=mesh_id,
        )

    def blk(r):
        return pl.ds(pl.multiple_of(r * span, span), span)

    def strip(r, lo, hi):
        return pl.ds(pl.multiple_of(r * width + lo, 16), hi - lo)

    loads = [
        pltpu.make_async_copy(src, dst, in_sem.at[i])
        for i, (src, dst) in enumerate([
            (mask_hbm, mask), (starts_hbm, starts), (refl_hbm, refl),
            (panels_hbm, panels), (cmap_hbm, cmap), (coeffs_hbm, coeffs)])
    ]
    for load in loads:
        load.start()

    barrier = pltpu.get_barrier_semaphore()
    for k in range(1, n):
        pl.semaphore_signal(barrier, inc=1, device_id=at_row((me + k) % n),
                            device_id_type=mesh_id)
    greeted = n - 1
    for d in (-2, -1, 1, 2):
        there = jnp.logical_and(front + d >= 0, front + d < fronts)
        greeted = greeted + jnp.where(there, 1, 0)

        @pl.when(there)
        def _(d=d):
            pl.semaphore_signal(barrier, inc=1, device_id=at_front(front + d),
                                device_id_type=mesh_id)

    for load in loads[:3]:
        load.wait()
    row_ids = me * span + lax.broadcasted_iota(jnp.int32, (span, LANES), 0)
    for j in range(refl.shape[2] // LANES):
        keep = jnp.logical_and(row_ids >= starts[0, j], mask[0, 0, j] == 1)
        block = refl[0, :, j * LANES:(j + 1) * LANES]
        ea[blk(me), j * LANES:(j + 1) * LANES] = jnp.where(keep, block, jnp.zeros_like(block))

    pl.semaphore_wait(barrier, greeted)

    e_out = []
    for k in range(1, chips):
        c = remote(ea.at[blk(me)], ea.at[blk(me)], e_send.at[k], e_recv.at[k],
                   at_row(((chip + k) % chips) * 2 + core))
        c.start()
        e_out.append(c)
    c = remote(ea.at[blk(me)], ea.at[blk(me)], s_send.at[0], s_recv.at[0], at_row(sibling))
    c.start()
    e_out.append(c)

    loads[3].wait()
    for j in range(cols // LANES):
        pt[j * LANES:(j + 1) * LANES, :] = panels[0, :, j * LANES:(j + 1) * LANES].T
    if pt.shape[0] > cols:
        pt[cols:, :] = jnp.zeros((pt.shape[0] - cols, span), BF16)
    p_out = []
    for h, (lo, hi) in enumerate(bounds):
        for k in range(1, n):
            peer = (me + k) % n
            c = remote(pt.at[strip(peer, lo, hi)], pr.at[pl.ds(lo, hi - lo), blk(me)],
                       p_send.at[h, k], p_recv.at[h, k], at_row(peer))
            c.start()
            p_out.append(c)
    pr[:, blk(me)] = pt[strip(me, 0, width), :]

    loads[4].wait()
    ncar = cmap.shape[1]
    targets = jnp.broadcast_to(cmap[...], (LANES, ncar)).T
    lane = lax.broadcasted_iota(jnp.int32, (ncar, LANES), 1)
    for b in range(rows // LANES):
        place[:, b * LANES:(b + 1) * LANES] = jnp.where(
            targets == lane + b * LANES, 1.0, 0.0).astype(BF16)
    loads[5].wait()

    for k in range(1, chips):
        src = ((chip + chips - k) % chips) * 2 + core
        e_out[k - 1].wait_recv()
        c = remote(ea.at[blk(src)], ea.at[blk(src)], s_send.at[k], s_recv.at[k], at_row(sibling))
        c.start()
        e_out.append(c)
    for c in e_out[chips - 1:]:
        c.wait_recv()

    even = front % 2 == 0
    has_next = front + 1 < fronts
    feeds = jnp.logical_and(even, has_next)
    feeds_map = jnp.logical_and(feeds, front > 0)
    odd_next = jnp.logical_and(front % 2 == 1, has_next)
    odd_after = jnp.logical_and(front % 2 == 1, front + 2 < fronts)
    odd_late = jnp.logical_and(front % 2 == 1, front > 1)
    even_late = jnp.logical_and(even, front > 0)

    m_copy = remote(step.at[:, pl.ds(tail, rows - tail)], step_in, m_send, m_recv,
                    at_front(lax.rem(front + 1, fronts)))

    t_copies, c_copies, d_copies, r_out = [], [], [], []
    for h, (lo, hi) in enumerate(bounds):
        part = pl.ds(lo, hi - lo)
        t_copies.append(remote(tails.at[part], tail_in.at[part], t_send.at[h], t_recv.at[h],
                               at_front(lax.rem(front + 1, fronts))))
        c_copies.append(remote(cout.at[part], cin.at[part], c_send.at[h], c_recv.at[h],
                               at_front(lax.rem(front + 1, fronts))))
        d_copies.append(remote(cout.at[part], cin.at[part], d_send.at[h], c_recv.at[h],
                               at_front(lax.rem(front + 2, fronts))))

    for h, (lo, hi) in enumerate(bounds):
        for c in p_out[h * (n - 1):(h + 1) * (n - 1)]:
            c.wait_recv()
        wcoef = dot(pr[lo:hi, :], ea[...]).astype(BF16)
        mix[lo:hi, :] = dot(wcoef, coeffs[0]).astype(BF16)
        own = pr[lo:hi, tail:].astype(F32) - dot_nt(mix[lo:hi, :], ea[tail:, :])
        tails[lo:hi, :] = own.astype(BF16)
        rest[lo:hi, tail:] = own

        @pl.when(feeds)
        def _(h=h):
            t_copies[h].start()

    ec = dot(place[...], ea[...]).astype(BF16)
    through = dot(ec, coeffs[0]).astype(BF16)

    def map_columns(lo, hi):
        step[:, lo:hi] = (place[:, lo:hi].astype(F32)
                          - dot_nt(through, ea[lo:hi, :])).astype(BF16)

    map_columns(tail, rows)

    @pl.when(feeds_map)
    def _():
        m_copy.start()

    def rest_rows(lo, hi):
        rest[lo:hi, :tail] = pr[lo:hi, :tail].astype(F32) - dot_nt(mix[lo:hi, :], ea[:tail, :])

    @pl.when(front == 0)
    def _():
        for lo, hi in bounds:
            rest_rows(lo, hi)

    @pl.when(front > 1)
    def _():
        map_columns(0, tail)
        rest_rows(0, width)

    for h, (lo, hi) in enumerate(bounds):
        @pl.when(front == 1)
        def _():
            t_copies[h].wait_recv()
            carry[lo:hi, :] = tail_in[lo:hi, :]

        @pl.when(even_late)
        def _():
            c_copies[h].wait_recv()
            carry[lo:hi, :] = cin[lo:hi, :]

        @pl.when(odd_late)
        def _():
            if h == 0:
                m_copy.wait_recv()
            t_copies[h].wait_recv()
            c_copies[h].wait_recv()
            carry[lo:hi, :] = (tail_in[lo:hi, :].astype(F32)
                               + dot(cin[lo:hi, :], step_in[...])).astype(BF16)

        @pl.when(odd_next)
        def _():
            cout[lo:hi, :] = (tails[lo:hi, :].astype(F32)
                              + dot(carry[lo:hi, :], step[:, tail:])).astype(BF16)

        @pl.when(odd_after)
        def _():
            d_copies[h].start()

        @pl.when(odd_next)
        def _():
            c_copies[h].start()

    @pl.when(front == 1)
    def _():
        map_columns(0, tail)
        rest_rows(0, width)

    for h, (lo, hi) in enumerate(bounds):
        @pl.when(front == 0)
        def _():
            rt[lo:hi, :] = rest[lo:hi, :].astype(BF16)

        @pl.when(front > 0)
        def _():
            rt[lo:hi, :] = (rest[lo:hi, :] + dot(carry[lo:hi, :], step[...])).astype(BF16)

        for k in range(1, n):
            peer = (me + k) % n
            c = remote(rt.at[pl.ds(lo, hi - lo), blk(peer)], rr.at[strip(me, lo, hi)],
                       r_send.at[h, k], r_recv.at[h, k], at_row(peer))
            c.start()
            r_out.append(c)
        rr[strip(me, lo, hi), :] = rt[lo:hi, blk(me)]

    for c in r_out:
        c.wait_recv()
    for j in range(cols // LANES):
        out_ref[0, :, j * LANES:(j + 1) * LANES] = rr[j * LANES:(j + 1) * LANES, :].T

    for c in e_out + p_out + r_out:
        c.wait_send()
    for flag, copies in ((feeds_map, [m_copy]), (feeds, t_copies),
                         (odd_after, d_copies), (odd_next, c_copies)):
        @pl.when(flag)
        def _(copies=copies):
            for c in copies:
                c.wait_send()


def local(n, fronts, panels, reflectors, block_coeffs, block_mask, block_starts, carry_map):
    _, span, cols = panels.shape
    k = reflectors.shape[2]
    rows = n * span
    ncar = carry_map.shape[1]
    width = -(-cols // (16 * n)) * 16
    half = width // 32 * 16
    bounds = ((0, half), (half, width))
    parts = len(bounds)
    dma = pltpu.SemaphoreType.DMA
    hbm = pl.BlockSpec(memory_space=pltpu.HBM)
    return pl.pallas_call(
        functools.partial(kernel, n, fronts, bounds, width),
        out_shape=jax.ShapeDtypeStruct(panels.shape, panels.dtype),
        in_specs=[hbm] * 6,
        out_specs=pl.BlockSpec(memory_space=pltpu.VMEM),
        scratch_shapes=[
            pltpu.SMEM(block_mask.shape, jnp.int32),
            pltpu.SMEM(block_starts.shape, jnp.int32),
            pltpu.VMEM(panels.shape, BF16),
            pltpu.VMEM(reflectors.shape, BF16),
            pltpu.VMEM(block_coeffs.shape, BF16),
            pltpu.VMEM(carry_map.shape, jnp.int32),
            pltpu.VMEM((n * width, span), BF16),
            pltpu.VMEM((width, rows), BF16),
            pltpu.VMEM((rows, k), BF16),
            pltpu.VMEM((ncar, rows), BF16),
            pltpu.VMEM((ncar, rows), BF16),
            pltpu.VMEM((ncar, ncar), BF16),
            pltpu.VMEM((width, ncar), BF16),
            pltpu.VMEM((width, ncar), BF16),
            pltpu.VMEM((width, ncar), BF16),
            pltpu.VMEM((width, ncar), BF16),
            pltpu.VMEM((width, ncar), BF16),
            pltpu.VMEM((width, k), BF16),
            pltpu.VMEM((width, rows), F32),
            pltpu.VMEM((width, rows), BF16),
            pltpu.VMEM((n * width, span), BF16),
            dma((6,)),
            dma((n // 2,)), dma((n // 2,)), dma((n // 2,)), dma((n // 2,)),
            dma((parts, n)), dma((parts, n)), dma((parts, n)), dma((parts, n)),
            dma((parts,)), dma((parts,)), dma((parts,)), dma((parts,)), dma((parts,)),
            dma, dma,
        ],
        compiler_params=pltpu.CompilerParams(
            collective_id=0, has_side_effects=True, vmem_limit_bytes=56 * 1024 * 1024),
    )(block_mask, block_starts, panels, reflectors, block_coeffs, carry_map)


def solution(mesh):
    in_specs = (
        P("front", "row", None),
        P("front", "row", None),
        P("front", None, None),
        P("front", "row", None),
        P("front", None),
        P("front", None),
    )
    body = functools.partial(local, mesh.shape["row"], mesh.shape["front"])
    return jax.shard_map(body, mesh=mesh, in_specs=in_specs,
                         out_specs=P("front", "row", None), check_vma=False)
```
